32 devices in a mesh: group: 2 (over x), lon: 16 (over z, y, core).
Axes of the slice: x: 2, y: 2, z: 4, core: 2. Of those that a mesh axis runs over, the one named last changes fastest.
Arguments:
- state: bfloat16 [32, 5, 2, 1440, 256], P('group', None, None, 'lon'), parts along dimension 0, may hold values from -6 to 6
- coefficients: bfloat16 [3, 2, 1440, 256], P(None, None, 'lon'), may hold values from -0.45 to 0.45, as said below
- counts: int32 [32], P('group'), parts along dimension 0, may hold values from 0 to 4, as said below
Outputs:
- analysis: bfloat16 [32, 5, 2, 1440, 256], P('group', None, None, 'lon'), parts along dimension 0
The draws below stay inside these ranges and needn't reach their ends.
There are 2 independent parts, one for each index of `group`. The reference program is written for one: setup_inputs(seed, part) draws one part's arguments, and reference() takes and returns one part's arrays. A program takes and returns all parts, laid end to end along the dimension named above; an argument that names none is the same for every part. Nothing has to cross between parts.
Inputs may be any that keep to these rules, and one draw needn't show every extreme that they name: The counts are non-negative and add up to 16; exactly one member has the largest count. `coefficients`: component 0 lies in the stated range; components 1 and 2 lie between 0.01 and 0.12.
All inputs are finite; a program needn't handle non-finite values.
Results may differ from the reference program's by a relative error of at most 0.0046.
Values may be sent and summed in bfloat16 or wider, within the bound.
A program may use at most 192 MiB of HBM per device.

```python
import math
import jax
import jax.numpy as jnp

MEMBERS = 16
FIELDS = 5
NLON = 1440
LEV = 2
YB = 256


def draw_coefficients(key, part):
    key = jax.random.fold_in(key, 7)
    first, second, third = jax.random.split(key, 3)
    shape = (LEV, NLON, YB)
    courant = jax.random.uniform(first, shape, jnp.float32, -0.45, 0.45)
    low = math.log(0.01)
    high = math.log(0.12)
    zonal = jnp.exp(jax.random.uniform(second, shape, jnp.float32, low, high))
    merid = jnp.exp(jax.random.uniform(third, shape, jnp.float32, low, high))
    return jnp.stack([courant, zonal, merid], axis=0).astype(jnp.bfloat16)


def draw_counts(key, part):
    key = jax.random.fold_in(key, 5)
    order_key, split_key = jax.random.split(key)
    order = jax.random.permutation(order_key, MEMBERS).astype(jnp.int32)
    pairs = (MEMBERS - 4) // 2
    shares = jax.random.randint(split_key, (pairs,), 0, 3).astype(jnp.int32)
    paired = jnp.stack([shares, 2 - shares], axis=1).reshape(2 * pairs)
    head = jnp.array([4, 0, 0, 0], dtype=jnp.int32)
    values = jnp.concatenate([head, paired], axis=0).astype(jnp.int32)
    return jnp.zeros((MEMBERS,), jnp.int32).at[order].set(values).astype(jnp.int32)


def shard_levels(stream_key, extent, cuts, least, largest):
    gain = 1.0
    for axis_at, blocks in cuts:
        heights = jax.random.uniform(jax.random.fold_in(jax.random.fold_in(stream_key, 6), axis_at), (blocks,), jnp.float32, least / len(cuts), largest / len(cuts))
        gain = gain * jnp.repeat(jnp.exp(heights), extent[axis_at] // blocks).reshape((-1,) + (1,) * (len(extent) - 1 - axis_at))
    return gain


def normal_values(key, extent, spread, most, cuts=(), kind=jnp.bfloat16):
    loudness = shard_levels(key, extent, cuts, -0.22, 0.18) if cuts else 1.0
    result = jax.random.normal(key, extent, jnp.float32) * spread * loudness
    return jnp.minimum(jnp.maximum(result, -most), most).astype(kind)


def setup_inputs(seed: int = 0, part: int = 0) -> dict:
    streams_of = jax.random.split(jax.random.key(seed), 4)
    part_keys = jax.random.split(jax.random.fold_in(streams_of[3], part), 4)
    state = normal_values(part_keys[0], (MEMBERS, FIELDS, LEV, NLON, YB), 1.0, 6.0, ((3, 16),))
    coefficients = draw_coefficients(jax.random.fold_in(streams_of[3], 71), part)
    counts = draw_counts(jax.random.fold_in(jax.random.fold_in(streams_of[3], part), 71), part)
    return {"state": state, "coefficients": coefficients, "counts": counts}


def minmod(first, second):
    return 0.5 * (jnp.sign(first) + jnp.sign(second)) * jnp.minimum(jnp.abs(first), jnp.abs(second))


def advance(extended, coefficients):
    n = extended.shape[-2]
    left = extended[..., 0:n - 2, :]
    middle = extended[..., 1:n - 1, :]
    right = extended[..., 2:n, :]
    slope = minmod(middle - left, right - middle)
    q_low = extended[..., 1:n - 2, :]
    q_high = extended[..., 2:n - 1, :]
    s_low = slope[..., 0:n - 3, :]
    s_high = slope[..., 1:n - 2, :]
    courant = coefficients[0]
    zonal = coefficients[1]
    merid = coefficients[2][:, 1:n - 3, :]
    flux = jnp.maximum(courant, 0.0) * (q_low + 0.5 * (1.0 - courant) * s_low) + jnp.minimum(courant, 0.0) * (q_high - 0.5 * (1.0 + courant) * s_high)
    total = zonal * (q_high - q_low) - flux
    count = total.shape[-2]
    zonal_change = total[..., 1:count, :] - total[..., 0:count - 1, :]
    center = extended[..., 2:n - 2, :]
    face_y = merid[..., :-1] * (center[..., 1:] - center[..., :-1])
    widths = [(0, 0)] * (face_y.ndim - 1)
    merid_change = jnp.pad(face_y, widths + [(0, 1)]) - jnp.pad(face_y, widths + [(1, 0)])
    return center + zonal_change + merid_change


def ancestors(counts):
    members = counts.shape[0]
    indices = jnp.arange(members, dtype=jnp.int32)
    losing = (counts == 0).astype(jnp.int32)
    ranking = jnp.cumsum(losing).astype(jnp.int32) - losing
    extras = jnp.cumsum(jnp.maximum(counts - 1, 0)).astype(jnp.int32)
    source = jnp.sum((extras[None, :] <= ranking[:, None]).astype(jnp.int32), axis=1).astype(jnp.int32)
    return jnp.where(counts > 0, indices, source).astype(jnp.int32)


def reference(state, coefficients, counts):
    faces = jnp.concatenate([coefficients[:, :, -1:, :], coefficients], axis=2).astype(jnp.float32)
    current = state
    for turn in range(2):
        extended = jnp.concatenate([current[..., -2:, :], current, current[..., :2, :]], axis=3).astype(jnp.float32)
        current = advance(extended, faces).astype(jnp.bfloat16)
    return jnp.take(current, ancestors(counts), axis=0)
```

```python
import functools

import jax
import jax.numpy as jnp
from jax import lax
from jax.experimental import pallas as pl
from jax.experimental.pallas import tpu as pltpu
from jax.sharding import PartitionSpec as P

HALO = 4


def ring(own, east, west, span):
    rows, lanes = own.shape
    zeros = jnp.zeros((span - rows - 2 * HALO, lanes), jnp.float32)
    return jnp.concatenate([own, east, zeros, west], axis=0)


def kernel(counts, state, coef, east, west, out, inbuf, outbuf, table, live, dead, in_sem, out_sem):
    members, slabs, rows, lanes = state.shape
    levels = coef.shape[1]
    span = table.shape[2]
    f32 = jnp.float32

    n_live = jnp.int32(0)
    n_dead = jnp.int32(0)
    for m in range(members):
        live[n_live] = m
        dead[n_dead] = m
        gone = (counts[m] == 0).astype(jnp.int32)
        n_dead = n_dead + gone
        n_live = n_live + 1 - gone

    def fetch(m):
        return pltpu.make_async_copy(state.at[m], inbuf.at[m], in_sem.at[m])

    def begin(i, carry):
        fetch(live[i]).start()
        return carry

    lax.fori_loop(0, n_live, begin, 0)

    column = lax.broadcasted_iota(jnp.int32, (span, lanes), 1)
    base = members * slabs
    for level in range(levels):
        c, kx, ky = (
            ring(
                coef[k, level].astype(f32),
                east[base + k * levels + level].astype(f32),
                west[base + k * levels + level].astype(f32),
                span,
            )
            for k in range(3)
        )
        up = jnp.maximum(c, 0.0)
        down = jnp.minimum(c, 0.0)
        ky = jnp.where(column == lanes - 1, 0.0, ky)
        ky_low = pltpu.roll(ky, 1, 1)
        table[level, 0] = 1.0 + pltpu.roll(c, 1, 0) - c - ky - ky_low
        table[level, 1] = kx - down
        table[level, 2] = -pltpu.roll(kx + up, 1, 0)
        table[level, 3] = ky
        table[level, 4] = ky_low
        table[level, 5] = -0.5 * up * (1.0 - c)
        table[level, 6] = 0.5 * down * (1.0 + c)

    def step(q, level):
        d = pltpu.roll(q, span - 1, 0) - q
        d_low = pltpu.roll(d, 1, 0)
        s = jnp.maximum(jnp.minimum(d, d_low), jnp.minimum(jnp.maximum(d, d_low), 0.0))
        n = table[level, 5] * s + table[level, 6] * pltpu.roll(s, span - 1, 0)
        total = table[level, 0] * q + table[level, 1] * d + table[level, 2] * d_low
        total = total + table[level, 3] * pltpu.roll(q, lanes - 1, 1)
        total = total + table[level, 4] * pltpu.roll(q, 1, 1)
        return total + (n - pltpu.roll(n, 1, 0))

    def member(i, used):
        m = live[i]
        fetch(m).wait()

        def slab(k, carry):
            level = lax.rem(k, levels)
            at = m * slabs + k
            q = ring(inbuf[m, k].astype(f32), east[at].astype(f32), west[at].astype(f32), span)
            q = step(q, level).astype(jnp.bfloat16).astype(f32)
            q = step(q, level)
            outbuf[m, k] = q[:rows].astype(jnp.bfloat16)
            return carry

        lax.fori_loop(0, slabs, slab, 0)
        pltpu.make_async_copy(outbuf.at[m], out.at[m], out_sem.at[m]).start()
        more = counts[m] - 1

        def extra(e, carry):
            to = dead[used + e]
            pltpu.make_async_copy(outbuf.at[m], out.at[to], out_sem.at[to]).start()
            return carry

        lax.fori_loop(0, more, extra, 0)
        return used + more

    lax.fori_loop(0, n_live, member, jnp.int32(0))
    for m in range(members):
        pltpu.make_async_copy(outbuf.at[m], out.at[m], out_sem.at[m]).wait()


def on_device(state, coefficients, counts):
    members, fields, levels, rows, lanes = state.shape
    slabs = fields * levels
    size = lax.axis_size("lon")
    up = [(i, (i + 1) % size) for i in range(size)]
    down = [(j, i) for i, j in up]

    def edge(start):
        a = lax.slice_in_dim(state, start, start + HALO, axis=3).reshape(members * slabs, HALO, lanes)
        b = lax.slice_in_dim(coefficients, start, start + HALO, axis=2).reshape(3 * levels, HALO, lanes)
        return jnp.concatenate([a, b], axis=0)

    west = lax.ppermute(edge(rows - HALO), "lon", up)
    east = lax.ppermute(edge(0), "lon", down)
    span = -(-(rows + 2 * HALO) // 8) * 8
    vmem = pl.BlockSpec(memory_space=pltpu.VMEM)
    out = pl.pallas_call(
        kernel,
        out_shape=jax.ShapeDtypeStruct((members, slabs, rows, lanes), state.dtype),
        in_specs=[
            pl.BlockSpec(memory_space=pltpu.SMEM),
            pl.BlockSpec(memory_space=pl.ANY),
            vmem,
            vmem,
            vmem,
        ],
        out_specs=pl.BlockSpec(memory_space=pl.ANY),
        scratch_shapes=[
            pltpu.VMEM((members, slabs, rows, lanes), jnp.bfloat16),
            pltpu.VMEM((members, slabs, rows, lanes), jnp.bfloat16),
            pltpu.VMEM((levels, 7, span, lanes), jnp.float32),
            pltpu.SMEM((members + 1,), jnp.int32),
            pltpu.SMEM((members + 1,), jnp.int32),
            pltpu.SemaphoreType.DMA((members,)),
            pltpu.SemaphoreType.DMA((members,)),
        ],
        compiler_params=pltpu.CompilerParams(vmem_limit_bytes=40 * 1024 * 1024),
        name="advance",
    )(counts, state.reshape(members, slabs, rows, lanes), coefficients, east, west)
    return out.reshape(state.shape)


def solution(mesh):
    return jax.shard_map(
        on_device,
        mesh=mesh,
        in_specs=(P("group", None, None, "lon", None), P(None, None, "lon", None), P("group")),
        out_specs=P("group", None, None, "lon", None),
        check_vma=False,
    )
```

```python
import jax
import jax.numpy as jnp
from jax import lax
from jax.experimental import pallas as pl
from jax.experimental.pallas import tpu as pltpu
from jax.sharding import PartitionSpec as P

HALO = 4
LANES = 128
PAD = 8
CHUNK = 48


def up_to_8(n):
    return -(-n // 8) * 8


def chunks(start, stop):
    return [(a, min(CHUNK, stop - a)) for a in range(start, stop, CHUNK)]


def kernel(counts, state, coef, east, west, out, inbuf, outbuf, table, ext, mid, flux, live, dead, in_sem, out_sem):
    members, fields, rows, _ = state.shape
    unit = east.shape[1] // HALO
    halo = east.shape[1]
    span = rows + 2 * halo
    f32 = jnp.float32

    n_live = jnp.int32(0)
    n_dead = jnp.int32(0)
    for m in range(members):
        live[n_live] = m
        dead[n_dead] = m
        gone = (counts[m] == 0).astype(jnp.int32)
        n_dead = n_dead + gone
        n_live = n_live + 1 - gone

    def fetch(m):
        return pltpu.make_async_copy(state.at[m], inbuf.at[m], in_sem.at[m])

    def begin(i, carry):
        fetch(live[i]).start()
        return carry

    lax.fori_loop(0, n_live, begin, 0)

    def sideways(x, ahead):
        tiles = x.reshape(x.shape[0] // 8, 8, LANES)
        lane = lax.broadcasted_iota(jnp.int32, tiles.shape, 2)
        turned = pltpu.roll(tiles, LANES - 1 if ahead else 1, 2)
        other = pltpu.roll(turned, 6 if ahead else 2, 1)
        return jnp.where(lane == (LANES - 1 if ahead else 0), other, turned).reshape(x.shape)

    zeros = jnp.zeros((PAD, LANES), f32)
    for ref in (ext, mid, flux):
        ref[0:PAD, :] = zeros
        ref[ref.shape[0] - 2 * PAD : ref.shape[0], :] = jnp.zeros((2 * PAD, LANES), f32)
    base = members * fields

    def load(target, own, k_own, k):
        target[PAD : PAD + halo, :] = west[k].astype(f32)
        for a, r in chunks(0, rows):
            target[PAD + halo + a : PAD + halo + a + r, :] = own[k_own + (pl.ds(a, r), slice(None))].astype(f32)
        target[PAD + halo + rows : PAD + span, :] = east[k].astype(f32)

    load(ext, coef, (0,), base)
    load(mid, coef, (1,), base + 1)
    load(flux, coef, (2,), base + 2)
    for a, r in chunks(0, up_to_8(span)):
        at = pl.ds(PAD + a, r)
        low = pl.ds(PAD + a - unit, r)
        c, kx, ky = ext[at, :], mid[at, :], flux[at, :]
        c_low, kx_low = ext[low, :], mid[low, :]
        row = lax.broadcasted_iota(jnp.int32, (r, LANES), 0)
        lane = lax.broadcasted_iota(jnp.int32, (r, LANES), 1)
        second = lax.rem(row, 4) >= 2
        ky_low = jnp.where(jnp.logical_and(jnp.logical_not(second), lane == 0), 0.0, sideways(ky, False))
        ky = jnp.where(jnp.logical_and(second, lane == LANES - 1), 0.0, ky)
        size = jnp.abs(c)
        table[0, pl.ds(a, r), :] = 1.0 + c_low - c - ky - ky_low
        table[1, pl.ds(a, r), :] = kx - jnp.minimum(c, 0.0)
        table[2, pl.ds(a, r), :] = -(kx_low + jnp.maximum(c_low, 0.0))
        table[3, pl.ds(a, r), :] = ky
        table[4, pl.ds(a, r), :] = ky_low
        table[5, pl.ds(a, r), :] = -0.5 * size * (1.0 - size)
        table[6, pl.ds(a, r), :] = c

    def limited(src, a, r):
        low = src[pl.ds(PAD + a - unit, r), :]
        q = src[pl.ds(PAD + a, r), :]
        high = src[pl.ds(PAD + a + unit, r), :]
        far = src[pl.ds(PAD + a + 2 * unit, r), :]
        d_low, d = q - low, high - q
        upwind = jnp.where(table[6, pl.ds(a, r), :] > 0.0, d_low, far - high)
        s = jnp.maximum(jnp.minimum(d, upwind), jnp.minimum(jnp.maximum(d, upwind), 0.0))
        n = table[5, pl.ds(a, r), :] * s
        flux[pl.ds(PAD + a, r), :] = n
        return q, d, d_low, n

    def advance(src, start, stop, store):
        limited(src, start - 8, 8)
        for a, r in chunks(start, start + up_to_8(stop - start)):
            q, d, d_low, n = limited(src, a, r)
            at = pl.ds(a, r)
            total = table[0, at, :] * q + table[1, at, :] * d + table[2, at, :] * d_low
            total = total + table[3, at, :] * sideways(q, True)
            total = total + table[4, at, :] * sideways(q, False)
            total = total + (n - flux[pl.ds(PAD + a - unit, r), :])
            store(a, r, total.astype(jnp.bfloat16))

    def member(i, used):
        m = live[i]
        fetch(m).wait()

        def field(k, carry):
            load(ext, inbuf, (m, k), m * fields + k)

            def middle(a, r, value):
                mid[pl.ds(PAD + a, r), :] = value.astype(f32)

            def last(a, r, value):
                r = min(r, halo + rows - a)
                outbuf[m, k, pl.ds(a - halo, r), :] = value[:r]

            advance(ext, halo // 2, span - halo // 2, middle)
            advance(mid, halo, halo + rows, last)
            return carry

        lax.fori_loop(0, fields, field, 0)
        pltpu.make_async_copy(outbuf.at[m], out.at[m], out_sem.at[m]).start()
        more = counts[m] - 1

        def extra(e, carry):
            to = dead[used + e]
            pltpu.make_async_copy(outbuf.at[m], out.at[to], out_sem.at[to]).start()
            return carry

        lax.fori_loop(0, more, extra, 0)
        return used + more

    lax.fori_loop(0, n_live, member, jnp.int32(0))
    for m in range(members):
        pltpu.make_async_copy(outbuf.at[m], out.at[m], out_sem.at[m]).wait()


def rowwise(x):
    head = x.shape[:-3]
    levels, sector, lat = x.shape[-3:]
    n = len(head)
    x = x.reshape(head + (levels, sector, lat // LANES, LANES))
    x = x.transpose(tuple(range(n)) + (n + 1, n + 2, n, n + 3))
    return x.reshape(head + (sector * (lat // LANES) * levels, LANES))


def on_device(state, coefficients, counts):
    members, fields, levels, sector, lat = state.shape
    size = lax.axis_size("lon")
    up = [(i, (i + 1) % size) for i in range(size)]
    down = [(j, i) for i, j in up]
    q = rowwise(state)
    coef = rowwise(coefficients)
    rows = q.shape[2]
    halo = HALO * levels * (lat // LANES)
    span = rows + 2 * halo

    def edge(start):
        a = lax.slice_in_dim(q, start, start + halo, axis=2).reshape(members * fields, halo, LANES)
        return jnp.concatenate([a, lax.slice_in_dim(coef, start, start + halo, axis=1)], axis=0)

    west = lax.ppermute(edge(rows - halo), "lon", up)
    east = lax.ppermute(edge(0), "lon", down)
    vmem = pl.BlockSpec(memory_space=pltpu.VMEM)
    out = pl.pallas_call(
        kernel,
        out_shape=jax.ShapeDtypeStruct(q.shape, q.dtype),
        in_specs=[
            pl.BlockSpec(memory_space=pltpu.SMEM),
            pl.BlockSpec(memory_space=pl.ANY),
            vmem,
            vmem,
            vmem,
        ],
        out_specs=pl.BlockSpec(memory_space=pl.ANY),
        scratch_shapes=[
            pltpu.VMEM(q.shape, jnp.bfloat16),
            pltpu.VMEM(q.shape, jnp.bfloat16),
            pltpu.VMEM((7, up_to_8(span), LANES), jnp.float32),
            pltpu.VMEM((up_to_8(span) + 2 * PAD, LANES), jnp.float32),
            pltpu.VMEM((up_to_8(span) + 2 * PAD, LANES), jnp.float32),
            pltpu.VMEM((up_to_8(span) + 2 * PAD, LANES), jnp.float32),
            pltpu.SMEM((members + 1,), jnp.int32),
            pltpu.SMEM((members + 1,), jnp.int32),
            pltpu.SemaphoreType.DMA((members,)),
            pltpu.SemaphoreType.DMA((members,)),
        ],
        compiler_params=pltpu.CompilerParams(vmem_limit_bytes=58 * 1024 * 1024),
        name="advance",
    )(counts, q, coef, east, west)
    out = out.reshape(members, fields, sector, lat // LANES, levels, LANES)
    return out.transpose(0, 1, 4, 2, 3, 5).reshape(state.shape)


def solution(mesh):
    return jax.shard_map(
        on_device,
        mesh=mesh,
        in_specs=(P("group", None, None, "lon", None), P(None, None, "lon", None), P("group")),
        out_specs=P("group", None, None, "lon", None),
        check_vma=False,
    )
```

```python
import jax
import jax.numpy as jnp
from jax import lax
from jax.experimental import pallas as pl
from jax.experimental.pallas import tpu as pltpu
from jax.sharding import PartitionSpec as P

HALO = 4
LANES = 128
PAD = 8
CHUNK = 48
f32 = jnp.float32


def up_to_8(n):
    return -(-n // 8) * 8


def chunks(start, stop):
    return [(a, min(CHUNK, stop - a)) for a in range(start, stop, CHUNK)]


def sideways(x, ahead):
    tiles = x.reshape(x.shape[0] // 8, 8, LANES)
    lane = lax.broadcasted_iota(jnp.int32, tiles.shape, 2)
    turned = pltpu.roll(tiles, LANES - 1 if ahead else 1, 2)
    other = pltpu.roll(turned, 6 if ahead else 2, 1)
    return jnp.where(lane == (LANES - 1 if ahead else 0), other, turned).reshape(x.shape)


def clear_pads(*refs):
    for ref in refs:
        ref[0:PAD, :] = jnp.zeros((PAD, LANES), f32)
        ref[ref.shape[0] - 2 * PAD : ref.shape[0], :] = jnp.zeros((2 * PAD, LANES), f32)


def combine(table, c_ref, kx_ref, ky_ref, span, unit):
    for a, r in chunks(0, up_to_8(span)):
        at = pl.ds(PAD + a, r)
        low = pl.ds(PAD + a - unit, r)
        c, kx, ky = c_ref[at, :], kx_ref[at, :], ky_ref[at, :]
        c_low, kx_low = c_ref[low, :], kx_ref[low, :]
        row = lax.broadcasted_iota(jnp.int32, (r, LANES), 0)
        lane = lax.broadcasted_iota(jnp.int32, (r, LANES), 1)
        second = lax.rem(row, 4) >= 2
        ky_low = jnp.where(jnp.logical_and(jnp.logical_not(second), lane == 0), 0.0, sideways(ky, False))
        ky = jnp.where(jnp.logical_and(second, lane == LANES - 1), 0.0, ky)
        size = jnp.abs(c)
        table[0, pl.ds(a, r), :] = 1.0 + c_low - c - ky - ky_low
        table[1, pl.ds(a, r), :] = kx - jnp.minimum(c, 0.0)
        table[2, pl.ds(a, r), :] = -(kx_low + jnp.maximum(c_low, 0.0))
        table[3, pl.ds(a, r), :] = ky
        table[4, pl.ds(a, r), :] = ky_low
        table[5, pl.ds(a, r), :] = -0.5 * size * (1.0 - size)
        table[6, pl.ds(a, r), :] = c


def limited(table, src, flux, a, r, unit):
    low = src[pl.ds(PAD + a - unit, r), :]
    q = src[pl.ds(PAD + a, r), :]
    high = src[pl.ds(PAD + a + unit, r), :]
    far = src[pl.ds(PAD + a + 2 * unit, r), :]
    d_low, d = q - low, high - q
    upwind = jnp.where(table[6, pl.ds(a, r), :] > 0.0, d_low, far - high)
    s = jnp.maximum(jnp.minimum(d, upwind), jnp.minimum(jnp.maximum(d, upwind), 0.0))
    n = table[5, pl.ds(a, r), :] * s
    flux[pl.ds(PAD + a, r), :] = n
    return q, d, d_low, n


def advance(table, src, flux, start, stop, unit, store):
    limited(table, src, flux, start - 8, 8, unit)
    for a, r in chunks(start, start + up_to_8(stop - start)):
        q, d, d_low, n = limited(table, src, flux, a, r, unit)
        at = pl.ds(a, r)
        total = table[0, at, :] * q + table[1, at, :] * d + table[2, at, :] * d_low
        total = total + table[3, at, :] * sideways(q, True)
        total = total + table[4, at, :] * sideways(q, False)
        total = total + (n - flux[pl.ds(PAD + a - unit, r), :])
        store(a, r, total.astype(jnp.bfloat16))


def interior(counts, state, coef, result, edges, inbuf, table, ext, mid, flux, live, in_sem):
    members, fields, rows, _ = state.shape
    side = edges.shape[3]
    unit = side // (2 * HALO)
    halo = side // 2

    n_live = jnp.int32(0)
    for m in range(members):
        live[n_live] = m
        n_live = n_live + (counts[m] != 0).astype(jnp.int32)

    def fetch(m):
        return pltpu.make_async_copy(state.at[m], inbuf.at[m], in_sem.at[m])

    def begin(i, carry):
        fetch(live[i]).start()
        return carry

    lax.fori_loop(0, n_live, begin, 0)
    clear_pads(ext, mid, flux)
    for k, ref in enumerate((ext, mid, flux)):
        for a, r in chunks(0, rows):
            ref[pl.ds(PAD + a, r), :] = coef[k, pl.ds(a, r), :].astype(f32)
    combine(table, ext, mid, flux, rows, unit)

    def member(i, carry):
        m = live[i]
        fetch(m).wait()

        def field(k, carry):
            for a, r in chunks(0, rows):
                ext[pl.ds(PAD + a, r), :] = inbuf[m, k, pl.ds(a, r), :].astype(f32)
            edges[m, k, 0] = ext[pl.ds(PAD, side), :]
            edges[m, k, 1] = ext[pl.ds(PAD + rows - side, side), :]

            def middle(a, r, value):
                mid[pl.ds(PAD + a, r), :] = value.astype(f32)

            def last(a, r, value):
                r = min(r, rows - halo - a)
                result[m, k, pl.ds(a, r), :] = value[:r]

            advance(table, ext, flux, halo // 2, rows - halo // 2, unit, middle)
            advance(table, mid, flux, halo, rows - halo, unit, last)
            return carry

        return lax.fori_loop(0, fields, field, carry)

    lax.fori_loop(0, n_live, member, 0)


def border(counts, _, edges, strips, east, west, out, result, table, ext, mid, flux, live, dead, out_sem):
    members, fields, rows, _ = result.shape
    side = edges.shape[3]
    halo = side // 2
    unit = halo // HALO
    span = side + halo
    base = members * fields

    n_live = jnp.int32(0)
    n_dead = jnp.int32(0)
    for m in range(members):
        live[n_live] = m
        dead[n_dead] = m
        gone = (counts[m] == 0).astype(jnp.int32)
        n_dead = n_dead + gone
        n_live = n_live + 1 - gone

    def join(ref, b, own, k):
        if b == 0:
            ref[PAD : PAD + halo, :] = west[k].astype(f32)
            ref[PAD + halo : PAD + span, :] = own
        else:
            ref[PAD : PAD + side, :] = own
            ref[PAD + side : PAD + span, :] = east[k].astype(f32)

    for b in range(2):
        refs = (ext.at[b], mid.at[b], flux.at[b])
        clear_pads(*refs)
        for k, ref in enumerate(refs):
            join(ref, b, strips[b, k].astype(f32), base + k)
        combine(table.at[b], *refs, span, unit)

    def member(i, used):
        m = live[i]

        def field(k, carry):
            for b in range(2):
                first, second, faces = ext.at[b], mid.at[b], flux.at[b]
                join(first, b, edges[m, k, b], m * fields + k)

                def middle(a, r, value):
                    second[pl.ds(PAD + a, r), :] = value.astype(f32)

                def last(a, r, value):
                    result[m, k, pl.ds((rows - halo) * b, halo), :] = value

                advance(table.at[b], first, faces, halo // 2, span - halo // 2, unit, middle)
                advance(table.at[b], second, faces, halo, 2 * halo, unit, last)
            return carry

        lax.fori_loop(0, fields, field, 0)
        pltpu.make_async_copy(result.at[m], out.at[m], out_sem.at[m]).start()
        more = counts[m] - 1

        def extra(e, carry):
            to = dead[used + e]
            pltpu.make_async_copy(result.at[m], out.at[to], out_sem.at[to]).start()
            return carry

        lax.fori_loop(0, more, extra, 0)
        return used + more

    lax.fori_loop(0, n_live, member, jnp.int32(0))
    for m in range(members):
        pltpu.make_async_copy(result.at[m], out.at[m], out_sem.at[m]).wait()


def rowwise(x):
    head = x.shape[:-3]
    levels, sector, lat = x.shape[-3:]
    n = len(head)
    x = x.reshape(head + (levels, sector, lat // LANES, LANES))
    x = x.transpose(tuple(range(n)) + (n + 1, n + 2, n, n + 3))
    return x.reshape(head + (sector * (lat // LANES) * levels, LANES))


def on_device(state, coefficients, counts):
    members, fields, levels, sector, lat = state.shape
    size = lax.axis_size("lon")
    up = [(i, (i + 1) % size) for i in range(size)]
    down = [(j, i) for i, j in up]
    q = rowwise(state)
    coef = rowwise(coefficients)
    rows = q.shape[2]
    halo = HALO * levels * (lat // LANES)

    def edge(start):
        a = lax.slice_in_dim(q, start, start + halo, axis=2).reshape(members * fields, halo, LANES)
        return jnp.concatenate([a, lax.slice_in_dim(coef, start, start + halo, axis=1)], axis=0)

    west = lax.ppermute(edge(rows - halo), "lon", up)
    east = lax.ppermute(edge(0), "lon", down)
    vmem = pl.BlockSpec(memory_space=pltpu.VMEM)
    smem = pl.BlockSpec(memory_space=pltpu.SMEM)
    anywhere = pl.BlockSpec(memory_space=pl.ANY)
    room = up_to_8(rows) + 2 * PAD
    result, edges = pl.pallas_call(
        interior,
        out_shape=[
            pltpu.VMEM(q.shape, jnp.bfloat16),
            pltpu.VMEM((members, fields, 2, 2 * halo, LANES), f32),
        ],
        in_specs=[smem, anywhere, vmem],
        out_specs=[vmem, vmem],
        scratch_shapes=[
            pltpu.VMEM(q.shape, jnp.bfloat16),
            pltpu.VMEM((7, up_to_8(rows), LANES), f32),
            pltpu.VMEM((room, LANES), f32),
            pltpu.VMEM((room, LANES), f32),
            pltpu.VMEM((room, LANES), f32),
            pltpu.SMEM((members + 1,), jnp.int32),
            pltpu.SemaphoreType.DMA((members,)),
        ],
        compiler_params=pltpu.CompilerParams(vmem_limit_bytes=46 * 1024 * 1024),
        cost_estimate=pl.CostEstimate(flops=40 * q.size, bytes_accessed=40 * q.size, transcendentals=0),
        name="interior",
    )(counts, q, coef)
    strips = jnp.stack([coef[:, : 2 * halo], coef[:, rows - 2 * halo :]])
    span = 3 * halo
    out, _ = pl.pallas_call(
        border,
        out_shape=[jax.ShapeDtypeStruct(q.shape, q.dtype), pltpu.VMEM(q.shape, q.dtype)],
        in_specs=[smem, vmem, vmem, vmem, vmem, vmem],
        out_specs=[anywhere, vmem],
        input_output_aliases={1: 1},
        scratch_shapes=[
            pltpu.VMEM((2, 7, span, LANES), f32),
            pltpu.VMEM((2, span + 2 * PAD, LANES), f32),
            pltpu.VMEM((2, span + 2 * PAD, LANES), f32),
            pltpu.VMEM((2, span + 2 * PAD, LANES), f32),
            pltpu.SMEM((members + 1,), jnp.int32),
            pltpu.SMEM((members + 1,), jnp.int32),
            pltpu.SemaphoreType.DMA((members,)),
        ],
        compiler_params=pltpu.CompilerParams(vmem_limit_bytes=24 * 1024 * 1024),
        name="border",
    )(counts, result, edges, strips, east, west)
    out = out.reshape(members, fields, sector, lat // LANES, levels, LANES)
    return out.transpose(0, 1, 4, 2, 3, 5).reshape(state.shape)


def solution(mesh):
    return jax.shard_map(
        on_device,
        mesh=mesh,
        in_specs=(P("group", None, None, "lon", None), P(None, None, "lon", None), P("group")),
        out_specs=P("group", None, None, "lon", None),
        check_vma=False,
    )
```

```python
import jax
import jax.numpy as jnp
from jax import lax
from jax.experimental import pallas as pl
from jax.experimental.pallas import tpu as pltpu
from jax.sharding import PartitionSpec as P

HALO = 4
LANES = 128
PAD = 8
CHUNK = 48
f32 = jnp.float32


def up_to_8(n):
    return -(-n // 8) * 8


def chunks(start, stop):
    return [(a, min(CHUNK, stop - a)) for a in range(start, stop, CHUNK)]


def sideways(x, ahead):
    tiles = x.reshape(x.shape[0] // 8, 8, LANES)
    lane = lax.broadcasted_iota(jnp.int32, tiles.shape, 2)
    turned = pltpu.roll(tiles, LANES - 1 if ahead else 1, 2)
    other = pltpu.roll(turned, 6 if ahead else 2, 1)
    return jnp.where(lane == (LANES - 1 if ahead else 0), other, turned).reshape(x.shape)


def clear_pads(*refs):
    for ref in refs:
        ref[0:PAD, :] = jnp.zeros((PAD, LANES), f32)
        ref[ref.shape[0] - 2 * PAD : ref.shape[0], :] = jnp.zeros((2 * PAD, LANES), f32)


def combine(table, c_ref, kx_ref, ky_ref, span, unit):
    for a, r in chunks(0, up_to_8(span)):
        at = pl.ds(PAD + a, r)
        low = pl.ds(PAD + a - unit, r)
        c, kx, ky = c_ref[at, :], kx_ref[at, :], ky_ref[at, :]
        c_low, kx_low = c_ref[low, :], kx_ref[low, :]
        row = lax.broadcasted_iota(jnp.int32, (r, LANES), 0)
        lane = lax.broadcasted_iota(jnp.int32, (r, LANES), 1)
        second = lax.rem(row, 4) >= 2
        ky_low = jnp.where(jnp.logical_and(jnp.logical_not(second), lane == 0), 0.0, sideways(ky, False))
        ky = jnp.where(jnp.logical_and(second, lane == LANES - 1), 0.0, ky)
        size = jnp.abs(c)
        table[0, pl.ds(a, r), :] = 1.0 + c_low - c - ky - ky_low
        table[1, pl.ds(a, r), :] = kx - jnp.minimum(c, 0.0)
        table[2, pl.ds(a, r), :] = -(kx_low + jnp.maximum(c_low, 0.0))
        table[3, pl.ds(a, r), :] = ky
        table[4, pl.ds(a, r), :] = ky_low
        table[5, pl.ds(a, r), :] = -0.5 * size * (1.0 - size)
        table[6, pl.ds(a, r), :] = c


def limited(table, src, flux, a, r, unit):
    low = src[pl.ds(PAD + a - unit, r), :]
    q = src[pl.ds(PAD + a, r), :]
    high = src[pl.ds(PAD + a + unit, r), :]
    far = src[pl.ds(PAD + a + 2 * unit, r), :]
    d_low, d = q - low, high - q
    upwind = jnp.where(table[6, pl.ds(a, r), :] > 0.0, d_low, far - high)
    s = jnp.maximum(jnp.minimum(d, upwind), jnp.minimum(jnp.maximum(d, upwind), 0.0))
    n = table[5, pl.ds(a, r), :] * s
    flux[pl.ds(PAD + a, r), :] = n
    return q, d, d_low, n


def advance(table, src, flux, start, stop, unit, store):
    limited(table, src, flux, start - 8, 8, unit)
    for a, r in chunks(start, start + up_to_8(stop - start)):
        q, d, d_low, n = limited(table, src, flux, a, r, unit)
        at = pl.ds(a, r)
        total = table[0, at, :] * q + table[1, at, :] * d + table[2, at, :] * d_low
        total = total + table[3, at, :] * sideways(q, True)
        total = total + table[4, at, :] * sideways(q, False)
        total = total + (n - flux[pl.ds(PAD + a - unit, r), :])
        store(a, r, total.astype(jnp.bfloat16))


def interior(counts, state, coef, result, edges, inbuf, table, ext, mid, flux, live, in_sem):
    members, fields, rows, _ = state.shape
    side = edges.shape[3]
    unit = side // (2 * HALO)
    halo = side // 2

    n_live = jnp.int32(0)
    for m in range(members):
        live[n_live] = m
        n_live = n_live + (counts[m] != 0).astype(jnp.int32)

    def fetch(m):
        return pltpu.make_async_copy(state.at[m], inbuf.at[m], in_sem.at[m])

    def begin(i, carry):
        fetch(live[i]).start()
        return carry

    lax.fori_loop(0, n_live, begin, 0)
    clear_pads(ext, mid, flux)
    for k, ref in enumerate((ext, mid, flux)):
        for a, r in chunks(0, rows):
            ref[pl.ds(PAD + a, r), :] = coef[k, pl.ds(a, r), :].astype(f32)
    combine(table, ext, mid, flux, rows, unit)

    def member(i, carry):
        m = live[i]
        fetch(m).wait()

        def field(k, carry):
            for a, r in chunks(0, rows):
                ext[pl.ds(PAD + a, r), :] = inbuf[m, k, pl.ds(a, r), :].astype(f32)
            edges[m, k, 0] = ext[pl.ds(PAD, side), :]
            edges[m, k, 1] = ext[pl.ds(PAD + rows - side, side), :]

            def middle(a, r, value):
                mid[pl.ds(PAD + a, r), :] = value.astype(f32)

            def last(a, r, value):
                r = min(r, rows - halo - a)
                result[m, k, pl.ds(a, r), :] = value[:r]

            advance(table, ext, flux, halo // 2, rows - halo // 2, unit, middle)
            advance(table, mid, flux, halo, rows - halo, unit, last)
            return carry

        return lax.fori_loop(0, fields, field, carry)

    lax.fori_loop(0, n_live, member, 0)


def border(counts, _, edges, strips, east, west, out, result, table, ext, mid, flux, live, dead, out_sem):
    members, fields, rows, _ = result.shape
    side = edges.shape[3]
    halo = side // 2
    unit = halo // HALO
    span = side + halo
    base = members * fields

    n_live = jnp.int32(0)
    n_dead = jnp.int32(0)
    for m in range(members):
        live[n_live] = m
        dead[n_dead] = m
        gone = (counts[m] == 0).astype(jnp.int32)
        n_dead = n_dead + gone
        n_live = n_live + 1 - gone

    def join(ref, b, own, k):
        if b == 0:
            ref[PAD : PAD + halo, :] = west[k].astype(f32)
            ref[PAD + halo : PAD + span, :] = own
        else:
            ref[PAD : PAD + side, :] = own
            ref[PAD + side : PAD + span, :] = east[k].astype(f32)

    for b in range(2):
        refs = (ext.at[b], mid.at[b], flux.at[b])
        clear_pads(*refs)
        for k, ref in enumerate(refs):
            join(ref, b, strips[b, k].astype(f32), base + k)
        combine(table.at[b], *refs, span, unit)
    for t in range(2, 2 * fields):
        clear_pads(ext.at[t], mid.at[t], flux.at[t])

    def member(i, used):
        m = live[i]

        for t in range(2 * fields):
            join(ext.at[t], t % 2, edges[m, t // 2, t % 2], m * fields + t // 2)
        for t in range(2 * fields):

            def middle(a, r, value):
                mid[t, pl.ds(PAD + a, r), :] = value.astype(f32)

            advance(table.at[t % 2], ext.at[t], flux.at[t], halo // 2, span - halo // 2, unit, middle)
        for t in range(2 * fields):

            def last(a, r, value):
                result[m, t // 2, pl.ds((rows - halo) * (t % 2), halo), :] = value

            advance(table.at[t % 2], mid.at[t], flux.at[fields * 2 + t], halo, 2 * halo, unit, last)
        pltpu.make_async_copy(result.at[m], out.at[m], out_sem.at[m]).start()
        more = counts[m] - 1

        def extra(e, carry):
            to = dead[used + e]
            pltpu.make_async_copy(result.at[m], out.at[to], out_sem.at[to]).start()
            return carry

        lax.fori_loop(0, more, extra, 0)
        return used + more

    lax.fori_loop(0, n_live, member, jnp.int32(0))
    for m in range(members):
        pltpu.make_async_copy(result.at[m], out.at[m], out_sem.at[m]).wait()


def rowwise(x):
    head = x.shape[:-3]
    levels, sector, lat = x.shape[-3:]
    n = len(head)
    x = x.reshape(head + (levels, sector, lat // LANES, LANES))
    x = x.transpose(tuple(range(n)) + (n + 1, n + 2, n, n + 3))
    return x.reshape(head + (sector * (lat // LANES) * levels, LANES))


def on_device(state, coefficients, counts):
    members, fields, levels, sector, lat = state.shape
    size = lax.axis_size("lon")
    up = [(i, (i + 1) % size) for i in range(size)]
    down = [(j, i) for i, j in up]
    q = rowwise(state)
    coef = rowwise(coefficients)
    rows = q.shape[2]
    halo = HALO * levels * (lat // LANES)

    def edge(start):
        a = lax.slice_in_dim(q, start, start + halo, axis=2).reshape(members * fields, halo, LANES)
        return jnp.concatenate([a, lax.slice_in_dim(coef, start, start + halo, axis=1)], axis=0)

    west = lax.ppermute(edge(rows - halo), "lon", up)
    east = lax.ppermute(edge(0), "lon", down)
    vmem = pl.BlockSpec(memory_space=pltpu.VMEM)
    smem = pl.BlockSpec(memory_space=pltpu.SMEM)
    anywhere = pl.BlockSpec(memory_space=pl.ANY)
    room = up_to_8(rows) + 2 * PAD
    result, edges = pl.pallas_call(
        interior,
        out_shape=[
            pltpu.VMEM(q.shape, jnp.bfloat16),
            pltpu.VMEM((members, fields, 2, 2 * halo, LANES), f32),
        ],
        in_specs=[smem, anywhere, vmem],
        out_specs=[vmem, vmem],
        scratch_shapes=[
            pltpu.VMEM(q.shape, jnp.bfloat16),
            pltpu.VMEM((7, up_to_8(rows), LANES), f32),
            pltpu.VMEM((room, LANES), f32),
            pltpu.VMEM((room, LANES), f32),
            pltpu.VMEM((room, LANES), f32),
            pltpu.SMEM((members + 1,), jnp.int32),
            pltpu.SemaphoreType.DMA((members,)),
        ],
        compiler_params=pltpu.CompilerParams(vmem_limit_bytes=46 * 1024 * 1024),
        cost_estimate=pl.CostEstimate(flops=40 * q.size, bytes_accessed=40 * q.size, transcendentals=0),
        name="interior",
    )(counts, q, coef)
    strips = jnp.stack([coef[:, : 2 * halo], coef[:, rows - 2 * halo :]])
    span = 3 * halo
    out, _ = pl.pallas_call(
        border,
        out_shape=[jax.ShapeDtypeStruct(q.shape, q.dtype), pltpu.VMEM(q.shape, q.dtype)],
        in_specs=[smem, vmem, vmem, vmem, vmem, vmem],
        out_specs=[anywhere, vmem],
        input_output_aliases={1: 1},
        scratch_shapes=[
            pltpu.VMEM((2, 7, span, LANES), f32),
            pltpu.VMEM((2 * fields, span + 2 * PAD, LANES), f32),
            pltpu.VMEM((2 * fields, span + 2 * PAD, LANES), f32),
            pltpu.VMEM((4 * fields, span + 2 * PAD, LANES), f32),
            pltpu.SMEM((members + 1,), jnp.int32),
            pltpu.SMEM((members + 1,), jnp.int32),
            pltpu.SemaphoreType.DMA((members,)),
        ],
        compiler_params=pltpu.CompilerParams(vmem_limit_bytes=24 * 1024 * 1024),
        name="border",
    )(counts, result, edges, strips, east, west)
    out = out.reshape(members, fields, sector, lat // LANES, levels, LANES)
    return out.transpose(0, 1, 4, 2, 3, 5).reshape(state.shape)


def solution(mesh):
    return jax.shard_map(
        on_device,
        mesh=mesh,
        in_specs=(P("group", None, None, "lon", None), P(None, None, "lon", None), P("group")),
        out_specs=P("group", None, None, "lon", None),
        check_vma=False,
    )
```

```python
import jax
import jax.numpy as jnp
from jax import lax
from jax.experimental import pallas as pl
from jax.experimental.pallas import tpu as pltpu
from jax.sharding import PartitionSpec as P

HALO = 4
LANES = 128
PAD = 8
CHUNK = 16
f32 = jnp.float32


def up_to_8(n):
    return -(-n // 8) * 8


def chunks(start, stop):
    return [(a, min(CHUNK, stop - a)) for a in range(start, stop, CHUNK)]


def sideways(x, ahead):
    tiles = x.reshape(x.shape[0] // 8, 8, LANES)
    lane = lax.broadcasted_iota(jnp.int32, tiles.shape, 2)
    turned = pltpu.roll(tiles, LANES - 1 if ahead else 1, 2)
    other = pltpu.roll(turned, 6 if ahead else 2, 1)
    return jnp.where(lane == (LANES - 1 if ahead else 0), other, turned).reshape(x.shape)


def clear_pads(*refs):
    for ref in refs:
        ref[0:PAD, :] = jnp.zeros((PAD, LANES), f32)
        ref[ref.shape[0] - 2 * PAD : ref.shape[0], :] = jnp.zeros((2 * PAD, LANES), f32)


def combine(table, c_ref, kx_ref, ky_ref, span, unit):
    for a, r in chunks(0, up_to_8(span)):
        at = pl.ds(PAD + a, r)
        low = pl.ds(PAD + a - unit, r)
        c, kx, ky = c_ref[at, :], kx_ref[at, :], ky_ref[at, :]
        c_low, kx_low = c_ref[low, :], kx_ref[low, :]
        row = lax.broadcasted_iota(jnp.int32, (r, LANES), 0)
        lane = lax.broadcasted_iota(jnp.int32, (r, LANES), 1)
        second = lax.rem(row, 4) >= 2
        ky_low = jnp.where(jnp.logical_and(jnp.logical_not(second), lane == 0), 0.0, sideways(ky, False))
        ky = jnp.where(jnp.logical_and(second, lane == LANES - 1), 0.0, ky)
        size = jnp.abs(c)
        table[0, pl.ds(a, r), :] = 1.0 + c_low - c - ky - ky_low
        table[1, pl.ds(a, r), :] = kx - jnp.minimum(c, 0.0)
        table[2, pl.ds(a, r), :] = -(kx_low + jnp.maximum(c_low, 0.0))
        table[3, pl.ds(a, r), :] = ky
        table[4, pl.ds(a, r), :] = ky_low
        table[5, pl.ds(a, r), :] = -0.5 * size * (1.0 - size)
        table[6, pl.ds(a, r), :] = c


def limited(slope, courant, src, flux, a, r, unit):
    low = src[pl.ds(PAD + a - unit, r), :]
    q = src[pl.ds(PAD + a, r), :]
    high = src[pl.ds(PAD + a + unit, r), :]
    far = src[pl.ds(PAD + a + 2 * unit, r), :]
    d_low, d = q - low, high - q
    upwind = jnp.where(courant > 0.0, d_low, far - high)
    s = jnp.maximum(jnp.minimum(d, upwind), jnp.minimum(jnp.maximum(d, upwind), 0.0))
    n = slope * s
    flux[pl.ds(PAD + a, r), :] = n
    return q, d, d_low, n


def advance(table, batch, start, stop, unit):
    at = pl.ds(start - 8, 8)
    slope, courant = table[5, at, :], table[6, at, :]
    for src, flux, _ in batch:
        limited(slope, courant, src, flux, start - 8, 8, unit)
    for a, r in chunks(start, start + up_to_8(stop - start)):
        at = pl.ds(a, r)
        c = [table[k, at, :] for k in range(7)]
        lane = lax.broadcasted_iota(jnp.int32, (r, LANES), 1)
        for src, flux, store in batch:
            q, d, d_low, n = limited(c[5], c[6], src, flux, a, r, unit)
            after = src[pl.ds(PAD + a + unit // 2, r), :]
            before = src[pl.ds(PAD + a - unit // 2, r), :]
            north = pltpu.roll(jnp.where(lane == 0, after, q), LANES - 1, 1)
            south = pltpu.roll(jnp.where(lane == LANES - 1, before, q), 1, 1)
            total = c[0] * q + c[1] * d + c[2] * d_low
            total = total + c[3] * north + c[4] * south
            total = total + (n - flux[pl.ds(PAD + a - unit, r), :])
            store(a, r, total.astype(jnp.bfloat16))


def interior(counts, state, coef, result, edges, inbuf, table, ext, mid, flux, live, in_sem):
    members, fields, rows, _ = state.shape
    side = edges.shape[3]
    unit = side // (2 * HALO)
    halo = side // 2

    n_live = jnp.int32(0)
    for m in range(members):
        live[n_live] = m
        n_live = n_live + (counts[m] != 0).astype(jnp.int32)

    def fetch(m):
        return pltpu.make_async_copy(state.at[m], inbuf.at[m], in_sem.at[m])

    def begin(i, carry):
        fetch(live[i]).start()
        return carry

    lax.fori_loop(0, n_live, begin, 0)
    for k in range(fields):
        clear_pads(ext.at[k], mid.at[k], flux.at[k])
    for k, ref in enumerate((ext.at[0], mid.at[0], flux.at[0])):
        for a, r in chunks(0, rows):
            ref[pl.ds(PAD + a, r), :] = coef[k, pl.ds(a, r), :].astype(f32)
    combine(table, ext.at[0], mid.at[0], flux.at[0], rows, unit)

    def member(i, carry):
        m = live[i]
        fetch(m).wait()

        def middle(k):
            def store(a, r, value):
                mid[k, pl.ds(PAD + a, r), :] = value.astype(f32)

            return store

        def last(k):
            def store(a, r, value):
                r = min(r, rows - halo - a)
                result[m, k, pl.ds(a, r), :] = value[:r]

            return store

        for k in range(fields):
            for a, r in chunks(0, rows):
                ext[k, pl.ds(PAD + a, r), :] = inbuf[m, k, pl.ds(a, r), :].astype(f32)
            edges[m, k, 0] = ext[k, pl.ds(PAD, side), :]
            edges[m, k, 1] = ext[k, pl.ds(PAD + rows - side, side), :]
        first = [(ext.at[k], flux.at[k], middle(k)) for k in range(fields)]
        advance(table, first, halo // 2, rows - halo // 2, unit)
        second = [(mid.at[k], flux.at[k], last(k)) for k in range(fields)]
        advance(table, second, halo, rows - halo, unit)
        return carry

    lax.fori_loop(0, n_live, member, 0)


def border(counts, _, edges, strips, east, west, out, result, table, ext, mid, flux, live, dead, out_sem):
    members, fields, rows, _ = result.shape
    side = edges.shape[3]
    halo = side // 2
    unit = halo // HALO
    span = side + halo
    base = members * fields

    n_live = jnp.int32(0)
    n_dead = jnp.int32(0)
    for m in range(members):
        live[n_live] = m
        dead[n_dead] = m
        gone = (counts[m] == 0).astype(jnp.int32)
        n_dead = n_dead + gone
        n_live = n_live + 1 - gone

    def join(ref, b, own, k):
        if b == 0:
            ref[PAD : PAD + halo, :] = west[k].astype(f32)
            ref[PAD + halo : PAD + span, :] = own
        else:
            ref[PAD : PAD + side, :] = own
            ref[PAD + side : PAD + span, :] = east[k].astype(f32)

    for b in range(2):
        refs = (ext.at[b], mid.at[b], flux.at[b])
        clear_pads(*refs)
        for k, ref in enumerate(refs):
            join(ref, b, strips[b, k].astype(f32), base + k)
        combine(table.at[b], *refs, span, unit)
    for t in range(2, 2 * fields):
        clear_pads(ext.at[t], mid.at[t], flux.at[t])

    def member(i, used):
        m = live[i]

        for t in range(2 * fields):
            join(ext.at[t], t % 2, edges[m, t // 2, t % 2], m * fields + t // 2)
        def middle(t):
            def store(a, r, value):
                mid[t, pl.ds(PAD + a, r), :] = value.astype(f32)

            return store

        def last(t):
            def store(a, r, value):
                result[m, t // 2, pl.ds((rows - halo) * (t % 2), halo), :] = value

            return store

        for b in range(2):
            strips_of = range(b, 2 * fields, 2)
            first = [(ext.at[t], flux.at[t], middle(t)) for t in strips_of]
            advance(table.at[b], first, halo // 2, span - halo // 2, unit)
        for b in range(2):
            strips_of = range(b, 2 * fields, 2)
            second = [(mid.at[t], flux.at[2 * fields + t], last(t)) for t in strips_of]
            advance(table.at[b], second, halo, 2 * halo, unit)
        pltpu.make_async_copy(result.at[m], out.at[m], out_sem.at[m]).start()
        more = counts[m] - 1

        def extra(e, carry):
            to = dead[used + e]
            pltpu.make_async_copy(result.at[m], out.at[to], out_sem.at[to]).start()
            return carry

        lax.fori_loop(0, more, extra, 0)
        return used + more

    lax.fori_loop(0, n_live, member, jnp.int32(0))
    for m in range(members):
        pltpu.make_async_copy(result.at[m], out.at[m], out_sem.at[m]).wait()


def rowwise(x):
    head = x.shape[:-3]
    levels, sector, lat = x.shape[-3:]
    n = len(head)
    x = x.reshape(head + (levels, sector, lat // LANES, LANES))
    x = x.transpose(tuple(range(n)) + (n + 1, n + 2, n, n + 3))
    return x.reshape(head + (sector * (lat // LANES) * levels, LANES))


def on_device(state, coefficients, counts):
    members, fields, levels, sector, lat = state.shape
    size = lax.axis_size("lon")
    up = [(i, (i + 1) % size) for i in range(size)]
    down = [(j, i) for i, j in up]
    q = rowwise(state)
    coef = rowwise(coefficients)
    rows = q.shape[2]
    halo = HALO * levels * (lat // LANES)

    def edge(start):
        a = lax.slice_in_dim(q, start, start + halo, axis=2).reshape(members * fields, halo, LANES)
        return jnp.concatenate([a, lax.slice_in_dim(coef, start, start + halo, axis=1)], axis=0)

    west = lax.ppermute(edge(rows - halo), "lon", up)
    east = lax.ppermute(edge(0), "lon", down)
    vmem = pl.BlockSpec(memory_space=pltpu.VMEM)
    smem = pl.BlockSpec(memory_space=pltpu.SMEM)
    anywhere = pl.BlockSpec(memory_space=pl.ANY)
    room = up_to_8(rows) + 2 * PAD
    result, edges = pl.pallas_call(
        interior,
        out_shape=[
            pltpu.VMEM(q.shape, jnp.bfloat16),
            pltpu.VMEM((members, fields, 2, 2 * halo, LANES), f32),
        ],
        in_specs=[smem, anywhere, vmem],
        out_specs=[vmem, vmem],
        scratch_shapes=[
            pltpu.VMEM(q.shape, jnp.bfloat16),
            pltpu.VMEM((7, up_to_8(rows), LANES), f32),
            pltpu.VMEM((fields, room, LANES), f32),
            pltpu.VMEM((fields, room, LANES), f32),
            pltpu.VMEM((fields, room, LANES), f32),
            pltpu.SMEM((members + 1,), jnp.int32),
            pltpu.SemaphoreType.DMA((members,)),
        ],
        compiler_params=pltpu.CompilerParams(vmem_limit_bytes=46 * 1024 * 1024),
        cost_estimate=pl.CostEstimate(flops=40 * q.size, bytes_accessed=40 * q.size, transcendentals=0),
        name="interior",
    )(counts, q, coef)
    strips = jnp.stack([coef[:, : 2 * halo], coef[:, rows - 2 * halo :]])
    span = 3 * halo
    out, _ = pl.pallas_call(
        border,
        out_shape=[jax.ShapeDtypeStruct(q.shape, q.dtype), pltpu.VMEM(q.shape, q.dtype)],
        in_specs=[smem, vmem, vmem, vmem, vmem, vmem],
        out_specs=[anywhere, vmem],
        input_output_aliases={1: 1},
        scratch_shapes=[
            pltpu.VMEM((2, 7, span, LANES), f32),
            pltpu.VMEM((2 * fields, span + 2 * PAD, LANES), f32),
            pltpu.VMEM((2 * fields, span + 2 * PAD, LANES), f32),
            pltpu.VMEM((4 * fields, span + 2 * PAD, LANES), f32),
            pltpu.SMEM((members + 1,), jnp.int32),
            pltpu.SMEM((members + 1,), jnp.int32),
            pltpu.SemaphoreType.DMA((members,)),
        ],
        compiler_params=pltpu.CompilerParams(vmem_limit_bytes=24 * 1024 * 1024),
        name="border",
    )(counts, result, edges, strips, east, west)
    out = out.reshape(members, fields, sector, lat // LANES, levels, LANES)
    return out.transpose(0, 1, 4, 2, 3, 5).reshape(state.shape)


def solution(mesh):
    return jax.shard_map(
        on_device,
        mesh=mesh,
        in_specs=(P("group", None, None, "lon", None), P(None, None, "lon", None), P("group")),
        out_specs=P("group", None, None, "lon", None),
        check_vma=False,
    )
```

```python
import jax
import jax.numpy as jnp
from jax import lax
from jax.experimental import pallas as pl
from jax.experimental.pallas import tpu as pltpu
from jax.sharding import PartitionSpec as P

HALO = 4
LANES = 128
PAD = 8
CHUNK = 16
f32 = jnp.float32


def up_to_8(n):
    return -(-n // 8) * 8


def chunks(start, stop):
    return [(a, min(CHUNK, stop - a)) for a in range(start, stop, CHUNK)]


def sideways(x, ahead):
    tiles = x.reshape(x.shape[0] // 8, 8, LANES)
    lane = lax.broadcasted_iota(jnp.int32, tiles.shape, 2)
    turned = pltpu.roll(tiles, LANES - 1 if ahead else 1, 2)
    other = pltpu.roll(turned, 6 if ahead else 2, 1)
    return jnp.where(lane == (LANES - 1 if ahead else 0), other, turned).reshape(x.shape)


def clear_pads(*refs):
    for ref in refs:
        ref[0:PAD, :] = jnp.zeros((PAD, LANES), f32)
        ref[ref.shape[0] - 2 * PAD : ref.shape[0], :] = jnp.zeros((2 * PAD, LANES), f32)


def combine(table, c_ref, kx_ref, ky_ref, span, unit):
    for a, r in chunks(0, up_to_8(span)):
        at = pl.ds(PAD + a, r)
        low = pl.ds(PAD + a - unit, r)
        c, kx, ky = c_ref[at, :], kx_ref[at, :], ky_ref[at, :]
        c_low, kx_low = c_ref[low, :], kx_ref[low, :]
        row = lax.broadcasted_iota(jnp.int32, (r, LANES), 0)
        lane = lax.broadcasted_iota(jnp.int32, (r, LANES), 1)
        second = lax.rem(row, 4) >= 2
        ky_low = jnp.where(jnp.logical_and(jnp.logical_not(second), lane == 0), 0.0, sideways(ky, False))
        ky = jnp.where(jnp.logical_and(second, lane == LANES - 1), 0.0, ky)
        size = jnp.abs(c)
        table[0, pl.ds(a, r), :] = 1.0 + c_low - c - ky - ky_low
        table[1, pl.ds(a, r), :] = kx - jnp.minimum(c, 0.0)
        table[2, pl.ds(a, r), :] = -(kx_low + jnp.maximum(c_low, 0.0))
        table[3, pl.ds(a, r), :] = ky
        table[4, pl.ds(a, r), :] = ky_low
        table[5, pl.ds(a, r), :] = -0.5 * size * (1.0 - size)
        table[6, pl.ds(a, r), :] = c


def limited(slope, courant, src, flux, a, r, unit):
    low = src[pl.ds(PAD + a - unit, r), :]
    q = src[pl.ds(PAD + a, r), :]
    high = src[pl.ds(PAD + a + unit, r), :]
    far = src[pl.ds(PAD + a + 2 * unit, r), :]
    d_low, d = q - low, high - q
    upwind = jnp.where(courant > 0.0, d_low, far - high)
    s = jnp.maximum(jnp.minimum(d, upwind), jnp.minimum(jnp.maximum(d, upwind), 0.0))
    n = slope * s
    flux[pl.ds(PAD + a, r), :] = n
    return q, d, d_low, n


def advance(table, batch, start, stop, unit):
    at = pl.ds(start - 8, 8)
    slope, courant = table[5, at, :], table[6, at, :]
    for src, flux, _ in batch:
        limited(slope, courant, src, flux, start - 8, 8, unit)
    for a, r in chunks(start, start + up_to_8(stop - start)):
        at = pl.ds(a, r)
        c = [table[k, at, :] for k in range(7)]
        lane = lax.broadcasted_iota(jnp.int32, (r, LANES), 1)
        for src, flux, store in batch:
            q, d, d_low, n = limited(c[5], c[6], src, flux, a, r, unit)
            after = src[pl.ds(PAD + a + unit // 2, r), :]
            before = src[pl.ds(PAD + a - unit // 2, r), :]
            north = pltpu.roll(jnp.where(lane == 0, after, q), LANES - 1, 1)
            south = pltpu.roll(jnp.where(lane == LANES - 1, before, q), 1, 1)
            total = c[0] * q + c[1] * d + c[2] * d_low
            total = total + c[3] * north + c[4] * south
            total = total + (n - flux[pl.ds(PAD + a - unit, r), :])
            store(a, r, total.astype(jnp.bfloat16))


def interior(counts, state, coef, result, edges, inbuf, table, ext, mid, flux, live, in_sem):
    members, fields, rows, _ = state.shape
    side = edges.shape[3]
    unit = side // (2 * HALO)
    halo = side // 2

    n_live = jnp.int32(0)
    for m in range(members):
        live[n_live] = m
        n_live = n_live + (counts[m] != 0).astype(jnp.int32)

    def fetch(m):
        return pltpu.make_async_copy(state.at[m], inbuf.at[m], in_sem.at[m])

    def begin(i, carry):
        fetch(live[i]).start()
        return carry

    lax.fori_loop(0, n_live, begin, 0)
    for k in range(fields):
        clear_pads(ext.at[k], mid.at[k], flux.at[k])
    for k, ref in enumerate((ext.at[0], mid.at[0], flux.at[0])):
        for a, r in chunks(0, rows):
            ref[pl.ds(PAD + a, r), :] = coef[k, pl.ds(a, r), :].astype(f32)
    combine(table, ext.at[0], mid.at[0], flux.at[0], rows, unit)

    def member(i, carry):
        m = live[i]
        fetch(m).wait()

        def middle(k):
            def store(a, r, value):
                mid[k, pl.ds(PAD + a, r), :] = value.astype(f32)

            return store

        def last(k):
            def store(a, r, value):
                r = min(r, rows - halo - a)
                result[m, k, pl.ds(a, r), :] = value[:r]

            return store

        for k in range(fields):
            for a, r in chunks(0, rows):
                ext[k, pl.ds(PAD + a, r), :] = inbuf[m, k, pl.ds(a, r), :].astype(f32)
            edges[m, k, 0] = ext[k, pl.ds(PAD, side), :]
            edges[m, k, 1] = ext[k, pl.ds(PAD + rows - side, side), :]
        first = [(ext.at[k], flux.at[k], middle(k)) for k in range(fields)]
        advance(table, first, halo // 2, rows - halo // 2, unit)
        second = [(mid.at[k], flux.at[k], last(k)) for k in range(fields)]
        advance(table, second, halo, rows - halo, unit)
        return carry

    lax.fori_loop(0, n_live, member, 0)


def border(counts, _, edges, coef, east, west, out, result, table, ext, mid, flux, live, dead, out_sem):
    members, fields, rows, _ = result.shape
    side = edges.shape[3]
    halo = side // 2
    unit = halo // HALO
    span = side + halo
    base = members * fields

    n_live = jnp.int32(0)
    n_dead = jnp.int32(0)
    for m in range(members):
        live[n_live] = m
        dead[n_dead] = m
        gone = (counts[m] == 0).astype(jnp.int32)
        n_dead = n_dead + gone
        n_live = n_live + 1 - gone

    def join(ref, b, own, k):
        if b == 0:
            ref[PAD : PAD + halo, :] = west[k].astype(f32)
            ref[PAD + halo : PAD + span, :] = own
        else:
            ref[PAD : PAD + side, :] = own
            ref[PAD + side : PAD + span, :] = east[k].astype(f32)

    for b in range(2):
        refs = (ext.at[b], mid.at[b], flux.at[b])
        clear_pads(*refs)
        for k, ref in enumerate(refs):
            join(ref, b, coef[k, pl.ds((rows - side) * b, side), :].astype(f32), base + k)
        combine(table.at[b], *refs, span, unit)
    for t in range(2, 2 * fields):
        clear_pads(ext.at[t], mid.at[t], flux.at[t])

    def member(i, used):
        m = live[i]

        for t in range(2 * fields):
            join(ext.at[t], t % 2, edges[m, t // 2, t % 2], m * fields + t // 2)
        def middle(t):
            def store(a, r, value):
                mid[t, pl.ds(PAD + a, r), :] = value.astype(f32)

            return store

        def last(t):
            def store(a, r, value):
                result[m, t // 2, pl.ds((rows - halo) * (t % 2), halo), :] = value

            return store

        for b in range(2):
            strips_of = range(b, 2 * fields, 2)
            first = [(ext.at[t], flux.at[t], middle(t)) for t in strips_of]
            advance(table.at[b], first, halo // 2, span - halo // 2, unit)
        for b in range(2):
            strips_of = range(b, 2 * fields, 2)
            second = [(mid.at[t], flux.at[2 * fields + t], last(t)) for t in strips_of]
            advance(table.at[b], second, halo, 2 * halo, unit)
        pltpu.make_async_copy(result.at[m], out.at[m], out_sem.at[m]).start()
        more = counts[m] - 1

        def extra(e, carry):
            to = dead[used + e]
            pltpu.make_async_copy(result.at[m], out.at[to], out_sem.at[to]).start()
            return carry

        lax.fori_loop(0, more, extra, 0)
        return used + more

    lax.fori_loop(0, n_live, member, jnp.int32(0))
    for m in range(members):
        pltpu.make_async_copy(result.at[m], out.at[m], out_sem.at[m]).wait()


def rowwise(x):
    head = x.shape[:-3]
    levels, sector, lat = x.shape[-3:]
    n = len(head)
    x = x.reshape(head + (levels, sector, lat // LANES, LANES))
    x = x.transpose(tuple(range(n)) + (n + 1, n + 2, n, n + 3))
    return x.reshape(head + (sector * (lat // LANES) * levels, LANES))


def on_device(state, coefficients, counts):
    members, fields, levels, sector, lat = state.shape
    size = lax.axis_size("lon")
    up = [(i, (i + 1) % size) for i in range(size)]
    down = [(j, i) for i, j in up]
    q = rowwise(state)
    coef = rowwise(coefficients)
    rows = q.shape[2]
    halo = HALO * levels * (lat // LANES)

    def edge(start):
        a = lax.slice_in_dim(q, start, start + halo, axis=2).reshape(members * fields, halo, LANES)
        return jnp.concatenate([a, lax.slice_in_dim(coef, start, start + halo, axis=1)], axis=0)

    west = lax.ppermute(edge(rows - halo), "lon", up)
    east = lax.ppermute(edge(0), "lon", down)
    vmem = pl.BlockSpec(memory_space=pltpu.VMEM)
    smem = pl.BlockSpec(memory_space=pltpu.SMEM)
    anywhere = pl.BlockSpec(memory_space=pl.ANY)
    room = up_to_8(rows) + 2 * PAD
    result, edges = pl.pallas_call(
        interior,
        out_shape=[
            pltpu.VMEM(q.shape, jnp.bfloat16),
            pltpu.VMEM((members, fields, 2, 2 * halo, LANES), f32),
        ],
        in_specs=[smem, anywhere, vmem],
        out_specs=[vmem, vmem],
        scratch_shapes=[
            pltpu.VMEM(q.shape, jnp.bfloat16),
            pltpu.VMEM((7, up_to_8(rows), LANES), f32),
            pltpu.VMEM((fields, room, LANES), f32),
            pltpu.VMEM((fields, room, LANES), f32),
            pltpu.VMEM((fields, room, LANES), f32),
            pltpu.SMEM((members + 1,), jnp.int32),
            pltpu.SemaphoreType.DMA((members,)),
        ],
        compiler_params=pltpu.CompilerParams(vmem_limit_bytes=46 * 1024 * 1024),
        cost_estimate=pl.CostEstimate(flops=40 * q.size, bytes_accessed=40 * q.size, transcendentals=0),
        name="interior",
    )(counts, q, coef)
    span = 3 * halo
    out, _ = pl.pallas_call(
        border,
        out_shape=[jax.ShapeDtypeStruct(q.shape, q.dtype), pltpu.VMEM(q.shape, q.dtype)],
        in_specs=[smem, vmem, vmem, vmem, vmem, vmem],
        out_specs=[anywhere, vmem],
        input_output_aliases={1: 1},
        scratch_shapes=[
            pltpu.VMEM((2, 7, span, LANES), f32),
            pltpu.VMEM((2 * fields, span + 2 * PAD, LANES), f32),
            pltpu.VMEM((2 * fields, span + 2 * PAD, LANES), f32),
            pltpu.VMEM((4 * fields, span + 2 * PAD, LANES), f32),
            pltpu.SMEM((members + 1,), jnp.int32),
            pltpu.SMEM((members + 1,), jnp.int32),
            pltpu.SemaphoreType.DMA((members,)),
        ],
        compiler_params=pltpu.CompilerParams(vmem_limit_bytes=24 * 1024 * 1024),
        name="border",
    )(counts, result, edges, coef, east, west)
    out = out.reshape(members, fields, sector, lat // LANES, levels, LANES)
    return out.transpose(0, 1, 4, 2, 3, 5).reshape(state.shape)


def solution(mesh):
    return jax.shard_map(
        on_device,
        mesh=mesh,
        in_specs=(P("group", None, None, "lon", None), P(None, None, "lon", None), P("group")),
        out_specs=P("group", None, None, "lon", None),
        check_vma=False,
    )
```
